256 devices in a mesh: row: 4 (over x), col: 4 (over y), slab: 16 (over z, core).
Axes of the slice: x: 4, y: 4, z: 8, core: 2. Of those that a mesh axis runs over, the one named last changes fastest.
Arguments:
- a_tiles: float32 [2048, 27, 4096], P(('row', 'col', 'slab')), may hold values from -0.75 to 0.75
- p_tiles: float32 [2048, 4096], P(('row', 'col', 'slab')), may hold values from -0.75 to 0.75
- col_ids: int32 [2048, 27], P(('row', 'col', 'slab')), may hold values from 0 to 2047, as said below
- row_tiles: int32 [2048], P(('row', 'col', 'slab')), may hold values from 1 to 27
- agg_ids: int32 [4, 4, 128], P(None, 'col'), may hold values from 0 to 7
- owner_map: int32 [4, 16, 8], P('col', 'slab'), may hold values from 0 to 7, each once within a row
Outputs:
- coarse: float32 [4, 4, 16, 2, 64, 1536], P('row', 'col', 'slab')
The draws below stay inside these ranges and needn't reach their ends.
Inputs may be any that keep to these rules, and one draw needn't show every extreme that they name: `col_ids`: slot 0 of each fine block names the block itself; every entry names a block with the same col index and a slab index that differs by at most 1. `owner_map`: each group's entries are a permutation.
All inputs are finite; a program needn't handle non-finite values.
Results may differ from the reference program's by a relative error of at most 0.0001.
Values sent between devices are 32-bit elements; how exact they have to be, the bound alone decides.
No kernel may reach another device: no remote copies, remote signals or barrier semaphores. Data moves between devices by JAX's collectives and lax.ppermute only.
A program may use at most 128 MiB of HBM per device.

```python
import jax
import jax.numpy as jnp
from jax import lax

B = 64
CW = 64
KT = 27
RB = 8
AG_DEV = 2
NPOOL = 8
NBLK = 2048
N_ROW = 4
N_COL = 4
N_SLAB = 16


def draw_col_ids(key, part):
    total = RB * N_ROW * N_COL * N_SLAB
    blocks = jnp.arange(total, dtype=jnp.int32)
    device = blocks // RB
    slab_of = device % N_SLAB
    col_of = device // N_SLAB % N_COL
    key_step = jax.random.fold_in(key, 11)
    key_row = jax.random.fold_in(key, 12)
    key_block = jax.random.fold_in(key, 13)
    step = jax.random.randint(key_step, (total, KT), -1, 2)
    target_slab = jnp.clip(slab_of[:, None] + step, 0, N_SLAB - 1)
    target_row = jax.random.randint(key_row, (total, KT), 0, N_ROW)
    target_block = jax.random.randint(key_block, (total, KT), 0, RB)
    chosen = ((target_row * N_COL + col_of[:, None]) * N_SLAB + target_slab) * RB + target_block
    chosen = chosen.at[:, 0].set(blocks)
    return chosen.astype(jnp.int32)


def set_ends(values, key, smallest, largest):
    dims = values.shape
    spot = [jax.random.randint(jax.random.fold_in(key, axis), (), 0, dims[axis]) for axis in range(len(dims))]
    values = values.at[tuple(spot)].set(smallest)
    longest = dims.index(max(dims))
    spot[longest] = (spot[longest] + 1) % dims[longest]
    return values.at[tuple(spot)].set(largest)


def block_scale(key, shape, shards, low, largest):
    gain = 1.0
    for dim, parts in shards:
        heights = jax.random.uniform(jax.random.fold_in(jax.random.fold_in(key, 6), dim), (parts,), jnp.float32, low / len(shards), largest / len(shards))
        gain = gain * jnp.repeat(jnp.exp(heights), shape[dim] // parts).reshape((-1,) + (1,) * (len(shape) - 1 - dim))
    return gain


def scatter_about(rng, dims, spread, bound, shards=(), kind=jnp.bfloat16):
    result = spread * jax.random.normal(rng, dims, jnp.float32)
    if shards:
        result = result * block_scale(rng, dims, shards, -0.22, 0.18)
    return jnp.clip(result, -bound, bound).astype(kind)


def setup_inputs(seed: int = 0) -> dict:
    keys = jax.random.split(jax.random.key(seed), 7)
    a_tiles = scatter_about(keys[0], (NBLK, KT, B * B), B ** -0.5, 0.75, ((0, 256),), jnp.float32)
    p_tiles = scatter_about(keys[1], (NBLK, B * CW), B ** -0.5, 0.75, ((0, 256),), jnp.float32)
    col_ids = draw_col_ids(jax.random.fold_in(keys[6], 71), 0)
    row_tiles = set_ends(jax.random.randint(keys[3], (NBLK,), 1, KT + 1), jax.random.fold_in(keys[3], 1), 1, KT).astype(jnp.int32)
    agg_ids = set_ends(jax.random.randint(keys[4], (N_ROW, N_COL, N_SLAB * RB), 0, NPOOL), jax.random.fold_in(keys[4], 1), 0, NPOOL - 1).astype(jnp.int32)
    owner_map = jax.vmap(lambda own: jax.random.permutation(own, NPOOL))(jax.random.split(keys[5], N_COL * N_SLAB)).reshape((N_COL, N_SLAB, NPOOL)).astype(jnp.int32)
    return {"a_tiles": a_tiles, "p_tiles": p_tiles, "col_ids": col_ids, "row_tiles": row_tiles, "agg_ids": agg_ids, "owner_map": owner_map}


def reference(a_tiles, p_tiles, col_ids, row_tiles, agg_ids, owner_map):
    npool = AG_DEV * N_ROW
    ncc = 3 * npool
    agg_flat = agg_ids.reshape(-1)
    highest = lax.Precision.HIGHEST

    def one_device(device):
        start = device * RB
        a_four = lax.dynamic_slice_in_dim(a_tiles, start, RB, 0).reshape(RB, KT, B, B)
        own_tiles = lax.dynamic_slice_in_dim(p_tiles, start, RB, 0).reshape(RB, B, CW)
        columns = lax.dynamic_slice_in_dim(col_ids, start, RB, 0).astype(jnp.int32)
        counts = lax.dynamic_slice_in_dim(row_tiles, start, RB, 0).astype(jnp.int32)
        far_tiles = p_tiles[columns].reshape(RB, KT, B, CW)
        left_prod = jnp.einsum('ixc,ikxy->ikcy', own_tiles, a_four, precision=highest)
        terms = jnp.einsum('ikcy,ikyd->ikcd', left_prod, far_tiles, precision=highest)
        live_mask = jnp.arange(KT, dtype=jnp.int32)[None, :] < counts[:, None]
        terms = jnp.where(live_mask[:, :, None, None], terms, jnp.zeros_like(terms))
        home_slab = device % N_SLAB
        own_agg = lax.dynamic_slice_in_dim(agg_flat, start, RB, 0).astype(jnp.int32)
        col_agg = agg_flat[columns].astype(jnp.int32)
        col_slab = (columns // RB) % N_SLAB
        slot = (col_slab - home_slab + 1) * npool + col_agg
        target = (own_agg[:, None] * ncc + slot).astype(jnp.int32)
        return jax.ops.segment_sum(terms.reshape(RB * KT, CW, CW), target.reshape(-1), num_segments=npool * ncc)

    def accumulate(device, total):
        device = jnp.asarray(device).astype(jnp.int32)
        partial_value = one_device(device)
        col_index = (device // N_SLAB) % N_COL
        slab_index = device % N_SLAB
        return total.at[col_index, slab_index].add(partial_value)

    total = jnp.zeros((N_COL, N_SLAB, npool * ncc, CW, CW), jnp.float32)
    total = lax.fori_loop(0, N_ROW * N_COL * N_SLAB, accumulate, total)
    inverse = jnp.argsort(owner_map, axis=-1).astype(jnp.int32)
    total = total.reshape(N_COL, N_SLAB, npool, ncc, CW, CW)
    ordered = jnp.take_along_axis(total, inverse[:, :, :, None, None, None], axis=2)
    ordered = ordered.reshape(N_COL, N_SLAB, N_ROW, AG_DEV, ncc, CW, CW)
    return ordered.transpose(2, 0, 1, 3, 5, 4, 6).reshape(N_ROW, N_COL, N_SLAB, AG_DEV, CW, ncc * CW)
```

```python
import functools

import jax
import jax.numpy as jnp
from jax import lax
from jax.experimental import pallas as pl
from jax.experimental.pallas import tpu as pltpu
from jax.sharding import PartitionSpec as P

B = 64
CW = 64
KT = 27
RB = 8
NPOOL = 8
N_ROW = 4
TILES = RB * KT
LIST = 224
UNROLL = 8
LEFT_UNROLL = 4
XP = 32
f32 = jnp.float32
bf16 = jnp.bfloat16


def split(x):
    hi = x.astype(bf16)
    return hi, (x - hi.astype(f32)).astype(bf16)


def left_kernel(
    sizes,
    a_ref,
    p_ref,
    cols,
    counts,
    aggs,
    owners,
    t_ref,
    mid_list,
    edge_list,
    lengths,
    p_buf,
):
    row_shift, slab_mask = sizes
    row = lax.axis_index("row")
    slab = lax.axis_index("slab")
    for x in range(XP):
        p_buf[pl.ds(x, RB, stride=XP), :] = p_ref[:, x * 128 : (x + 1) * 128]
    first = lax.broadcasted_iota(jnp.int32, (XP, 128), 1) < 64
    first_out = lax.broadcasted_iota(jnp.int32, (CW, 128), 1) < 64

    def block(i, lengths):
        packed = p_buf[pl.ds(pl.multiple_of(i * XP, XP), XP), :]
        own = jnp.concatenate([packed[:, :64], packed[:, 64:]], axis=0)
        hi, lo = split(own.T)
        lhs = jnp.concatenate([hi, hi, lo], axis=1)
        count = counts[i]
        position = owners[0, 0, aggs[row, 0, slab * RB + i]]
        place = (((position >> 1) - row) & (N_ROW - 1)) * 2 + (position & 1)

        def tiles(n, lengths):
            mid_length, edge_length = lengths
            for u in range(LEFT_UNROLL):
                k = jnp.minimum(n * LEFT_UNROLL + u, KT - 1)
                a = a_ref[pl.ds(k * (XP * RB) + i, XP, stride=RB), :]
                turned = pltpu.roll(a, 64, 1)
                two = jnp.concatenate(
                    [jnp.where(first, a, turned), jnp.where(first, turned, a)], axis=0
                )
                a_hi, a_lo = split(two)
                rhs = jnp.concatenate([a_hi, a_lo, a_hi], axis=0)
                t = jnp.dot(lhs, rhs, preferred_element_type=f32)
                rest = t - t.astype(bf16).astype(f32)
                t_ref[k * RB + i] = jnp.where(first_out, t, rest).astype(bf16)

                source = cols[i, k]
                source_slab = (source >> 3) & slab_mask
                source_row = source >> row_shift
                source_block = source & (RB - 1)
                agg = aggs[source_row, 0, source_slab * RB + source_block]
                panel = ((source_row - row) & (N_ROW - 1)) * RB + source_block
                step = source_slab - slab
                upper = jnp.maximum(step, 0)
                base = k * RB + i + (panel << 8)
                mid_list[mid_length] = base + ((place * 4 + (agg >> 1)) << 16)
                edge_list[edge_length] = (
                    base
                    + (upper << 13)
                    + ((place * 8 + upper * 4 + (agg >> 1)) << 16)
                )
                live = (n * LEFT_UNROLL + u < count).astype(jnp.int32)
                is_mid = (step == 0).astype(jnp.int32)
                mid_length = mid_length + live * is_mid
                edge_length = edge_length + live * (1 - is_mid)
            return mid_length, edge_length

        rounds = (count + LEFT_UNROLL - 1) // LEFT_UNROLL
        return lax.fori_loop(0, rounds, tiles, lengths)

    zero = jnp.int32(0)
    mid_length, edge_length = lax.fori_loop(0, RB, block, (zero, zero))
    for u in range(UNROLL):
        mid_list[mid_length + u] = 32 << 16
        edge_list[edge_length + u] = 64 << 16
    lengths[0] = mid_length
    lengths[1] = edge_length


def left_products(a_tiles, p_tiles, col_ids, row_tiles, agg_ids, owner_map):
    n_col, n_slab = lax.axis_size("col"), lax.axis_size("slab")
    sizes = ((RB * n_col * n_slab).bit_length() - 1, n_slab - 1)
    rows = a_tiles.transpose(1, 0, 2).reshape(KT, RB, XP, 128)
    rows = rows.transpose(0, 2, 1, 3).reshape(KT * XP * RB, 128)
    vmem = pl.BlockSpec(memory_space=pltpu.VMEM)
    smem = pl.BlockSpec(memory_space=pltpu.SMEM)
    return pl.pallas_call(
        functools.partial(left_kernel, sizes),
        out_shape=[
            jax.ShapeDtypeStruct((TILES, CW, 128), bf16),
            jax.ShapeDtypeStruct((LIST,), jnp.int32),
            jax.ShapeDtypeStruct((LIST,), jnp.int32),
            jax.ShapeDtypeStruct((2,), jnp.int32),
        ],
        in_specs=[vmem, vmem, smem, smem, smem, smem],
        out_specs=[vmem, smem, smem, smem],
        scratch_shapes=[pltpu.VMEM((RB * XP, 128), f32)],
        compiler_params=pltpu.CompilerParams(vmem_limit_bytes=24 << 20),
        cost_estimate=pl.CostEstimate(
            flops=4_000_000_000, bytes_accessed=8_000_000, transcendentals=0
        ),
        name="left_products",
    )(rows, p_tiles, col_ids, row_tiles, agg_ids, owner_map)


def right_kernel(which, n_slab, n_blocks, pairs, *refs):
    todo, lengths, aggs, t_hbm = refs[:4]
    p_refs = refs[4 : 4 + n_blocks]
    outs = refs[4 + n_blocks : 12 + n_blocks]
    t_buf, flat, panel, acc, sem, out_sem = refs[12 + n_blocks :]
    load = pltpu.make_async_copy(t_hbm, t_buf, sem)
    load.start()
    row = lax.axis_index("row")
    slab = lax.axis_index("slab")
    left = lax.broadcasted_iota(jnp.int32, (RB, 128), 1) < 64
    sub = lax.broadcasted_iota(jnp.int32, (RB, 128), 0)
    blocks = [ref.at[pl.ds(n, RB)] for ref in p_refs for n in range(0, ref.shape[0], RB)]
    for b, block in enumerate(blocks):
        shift = 0 if which == 0 else 2 * (b // N_ROW) - 1
        near_slab = jnp.clip(slab + shift, 0, n_slab - 1)
        near_row = (row + b) & (N_ROW - 1)
        odd = jnp.zeros((RB, 128), jnp.int32)
        for i in range(RB):
            odd = jnp.where(sub == i, aggs[near_row, 0, near_slab * RB + i], odd)
        odd = (odd & 1) == 1
        keep_even = jnp.logical_and(left, jnp.logical_not(odd))
        keep_odd = jnp.logical_and(jnp.logical_not(left), odd)
        for y in range(0, B, 2):
            v = block[:, y * 64 : y * 64 + 128]
            w = pltpu.roll(v, 64, 1)
            zero = jnp.zeros_like(v)
            flat[pl.ds(b * RB * B + y, RB, stride=B), :] = jnp.where(
                keep_even, v, jnp.where(keep_odd, w, zero)
            )
            flat[pl.ds(b * RB * B + y + 1, RB, stride=B), :] = jnp.where(
                keep_odd, v, jnp.where(keep_even, w, zero)
            )

    def prepare(m, carry):
        hi, lo = split(flat[pl.ds(pl.multiple_of(m * B, B), B), :])
        panel[m, :, :128] = hi
        panel[m, :, 128:] = lo
        return carry

    lax.fori_loop(0, len(blocks) * RB, prepare, 0, unroll=4)
    acc[...] = jnp.zeros_like(acc)
    load.wait()

    def step(n, carry):
        for u in range(UNROLL):
            value = todo[n * UNROLL + u]
            w = panel[(value >> 8) & 255]
            o = jnp.dot(
                t_buf[value & 255],
                jnp.concatenate([w, w], axis=0),
                preferred_element_type=f32,
            )
            acc[value >> 16] += o[:, :128] + o[:, 128:]
        return carry

    lax.fori_loop(0, (lengths[which] + UNROLL - 1) // UNROLL, step, 0)
    copies = [
        pltpu.make_async_copy(acc.at[pl.ds(n * pairs, pairs)], outs[n], out_sem)
        for n in range(8)
    ]
    for copy in copies:
        copy.start()
    for copy in copies:
        copy.wait()


def right_products(which, todo, lengths, agg_ids, t, p_blocks):
    n = len(p_blocks)
    count = sum(x.shape[0] for x in p_blocks)
    pairs = count // 8
    vmem = pl.BlockSpec(memory_space=pltpu.VMEM)
    smem = pl.BlockSpec(memory_space=pltpu.SMEM)
    anywhere = pl.BlockSpec(memory_space=pl.ANY)
    return pl.pallas_call(
        functools.partial(right_kernel, which, lax.axis_size("slab"), n, pairs),
        out_shape=[jax.ShapeDtypeStruct((pairs, CW, 128), f32)] * 8,
        in_specs=[smem, smem, smem, anywhere] + [vmem] * n,
        out_specs=[anywhere] * 8,
        scratch_shapes=[
            pltpu.VMEM((TILES, CW, 128), bf16),
            pltpu.VMEM((count * B, 128), f32),
            pltpu.VMEM((count, B, 256), bf16),
            pltpu.VMEM((8 * pairs + 1, CW, 128), f32),
            pltpu.SemaphoreType.DMA,
            pltpu.SemaphoreType.DMA,
        ],
        compiler_params=pltpu.CompilerParams(vmem_limit_bytes=24 << 20),
        cost_estimate=pl.CostEstimate(
            flops=2_000_000_000, bytes_accessed=5_000_000, transcendentals=0
        ),
        name="right_products",
    )(todo, lengths, agg_ids, t, *p_blocks)


def finish_kernel(*refs):
    out = refs[-1]
    for t in range(2):
        mid = refs[6 * t : 6 * t + 3]
        edge = refs[6 * t + 3 : 6 * t + 6]
        for q in range(12):
            if 4 <= q < 8:
                value = mid[0][q - 4] + mid[1][q - 4] + mid[2][q - 4]
            else:
                e = q if q < 4 else q - 4
                value = edge[0][e] + edge[1][e] + edge[2][e]
            out[t, :, q * 128 : (q + 1) * 128] = value


def finish(parts):
    vmem = pl.BlockSpec(memory_space=pltpu.VMEM)
    return pl.pallas_call(
        finish_kernel,
        out_shape=jax.ShapeDtypeStruct((2, CW, 24 * CW), f32),
        in_specs=[vmem] * 12,
        out_specs=vmem,
        compiler_params=pltpu.CompilerParams(vmem_limit_bytes=24 << 20),
        name="finish",
    )(*parts)


def on_device(a_tiles, p_tiles, col_ids, row_tiles, agg_ids, owner_map):
    n_slab = lax.axis_size("slab")
    ring = lambda step: [(i, (i + step) % N_ROW) for i in range(N_ROW)]
    line = lambda step: [
        (i, i + step) for i in range(n_slab) if 0 <= i + step < n_slab
    ]
    up = lambda x: lax.ppermute(x, "row", ring(1))
    down = lambda x: lax.ppermute(x, "row", ring(-1))

    from_far = lax.ppermute(p_tiles, "row", ring(2))
    from_below = up(p_tiles)
    from_above = down(p_tiles)
    mid_blocks = [p_tiles, from_above, from_far, from_below]
    stacked = jnp.concatenate(mid_blocks, axis=0)
    from_lower = lax.ppermute(stacked, "slab", line(1))
    from_upper = lax.ppermute(stacked, "slab", line(-1))

    t, mid_list, edge_list, lengths = left_products(
        a_tiles, p_tiles, col_ids, row_tiles, agg_ids, owner_map
    )

    def reduce_to_owner(own0, own1, a0, a1, f0, f1, b0, b1):
        f0_in = up(f0)
        f1_in = down(f1)
        a1_in = up(a1)
        b0_in = down(b0)
        a0_in = up(a0 + f0_in)
        b1_in = down(b1 + f1_in)
        return (own0, a0_in, b0_in), (own1, a1_in, b1_in)

    mid = right_products(0, mid_list, lengths, agg_ids, t, mid_blocks)
    mid0, mid1 = reduce_to_owner(*mid)
    edge = right_products(
        1, edge_list, lengths, agg_ids, t, [from_lower, from_upper]
    )
    edge0, edge1 = reduce_to_owner(*edge)
    out = finish([*mid0, *edge0, *mid1, *edge1])
    return out.reshape(1, 1, 1, 2, CW, 24 * CW)


def solution(mesh):
    placed = (
        P(("row", "col", "slab"), None, None),
        P(("row", "col", "slab"), None),
        P(("row", "col", "slab"), None),
        P(("row", "col", "slab")),
        P(None, "col", None),
        P("col", "slab", None),
    )
    return jax.shard_map(
        on_device,
        mesh=mesh,
        in_specs=placed,
        out_specs=P("row", "col", "slab", None, None, None),
        check_vma=False,
    )
```

```python
import functools

import jax
import jax.numpy as jnp
from jax import lax
from jax.experimental import pallas as pl
from jax.experimental.pallas import tpu as pltpu
from jax.sharding import PartitionSpec as P

B = 64
CW = 64
KT = 27
RB = 8
NPOOL = 8
N_ROW = 4
UNROLL = 8
TILES = RB * KT
PAIRS = NPOOL // 2
LIST = TILES + UNROLL
GROUP = 3
XP = 32
PLACES = ((0, 1), (4, 3), (5, 6), (2,), (7,))
f32 = jnp.float32
bf16 = jnp.bfloat16


def split(x):
    hi = x.astype(bf16)
    return hi, (x - hi.astype(f32)).astype(bf16)


def in_hbm(x):
    return pltpu.with_memory_space_constraint(x, pltpu.HBM)


def left_kernel(
    n_slab,
    a_hbm,
    p_hbm,
    cols_hbm,
    counts_hbm,
    aggs_hbm,
    owners_hbm,
    t_ref,
    todo,
    a_buf,
    p_in,
    p_buf,
    lhs_buf,
    cols,
    counts,
    aggs,
    owners,
    a_sem,
    sem,
):
    small = [
        pltpu.make_async_copy(source, target, sem.at[n])
        for n, (source, target) in enumerate(
            [
                (p_hbm, p_in),
                (cols_hbm, cols),
                (counts_hbm, counts),
                (aggs_hbm, aggs),
                (owners_hbm, owners),
            ]
        )
    ]
    rows = GROUP * XP * RB

    def fetch(n):
        part = pl.ds(n * rows, rows)
        return pltpu.make_async_copy(a_hbm.at[part], a_buf.at[part], a_sem.at[n])

    for copy in small:
        copy.start()
    for n in range(KT // GROUP):
        fetch(n).start()
    for copy in small:
        copy.wait()
    row = lax.axis_index("row")
    slab = lax.axis_index("slab")
    for x in range(XP):
        p_buf[pl.ds(x, RB, stride=XP), :] = p_in[:, x * 128 : (x + 1) * 128]
    first = lax.broadcasted_iota(jnp.int32, (XP, 128), 1) < 64
    first_out = lax.broadcasted_iota(jnp.int32, (CW, 128), 1) < 64
    places = []
    for i in range(RB):
        packed = p_buf[i * XP : (i + 1) * XP, :]
        own = jnp.concatenate([packed[:, :64], packed[:, 64:]], axis=0)
        hi, lo = split(own.T)
        lhs_buf[i] = jnp.concatenate([hi, hi, lo, lo], axis=1)
        position = owners[0, 0, aggs[row, 0, slab * RB + i]]
        places.append((((position >> 1) - row) & (N_ROW - 1)) * 2 + (position & 1))

    def group(n, lengths):
        fetch(n).wait()
        own_at, pair_at, far_at = lengths
        entries = []
        for i in range(RB):
            for u in range(GROUP):
                k = n * GROUP + u
                source = cols[i, k]
                source_slab = (source >> 3) & (n_slab - 1)
                entries.append(
                    (
                        (source << 8) + (k * RB + i + (places[i] << 19)),
                        source_slab == slab,
                        source_slab == slab ^ 1,
                        k < counts[i],
                    )
                )
        for entry, is_own, is_pair, live in entries:
            todo[jnp.where(is_own, own_at, jnp.where(is_pair, pair_at, far_at))] = entry
            one = live.astype(jnp.int32)
            own_one = jnp.where(is_own, one, 0)
            pair_one = jnp.where(is_pair, one, 0)
            own_at = own_at + own_one
            pair_at = pair_at + pair_one
            far_at = far_at + (one - own_one - pair_one)
        for i in range(RB):
            lhs = lhs_buf[i]
            parts = []
            for u in range(GROUP):
                k = n * GROUP + u
                a = a_buf[pl.ds(k * (XP * RB) + i, XP, stride=RB), :]
                turned = pltpu.roll(a, 64, 1)
                two = jnp.concatenate(
                    [jnp.where(first, a, turned), jnp.where(first, turned, a)], axis=0
                )
                hi, lo = split(two)
                parts.append(jnp.concatenate([hi, lo, hi, lo], axis=0))

            t = jnp.dot(
                lhs, jnp.concatenate(parts, axis=1), preferred_element_type=f32
            )
            for u in range(GROUP):
                one = t[:, u * 128 : (u + 1) * 128]
                rest = one - one.astype(bf16).astype(f32)
                t_ref[(n * GROUP + u) * RB + i] = jnp.where(
                    first_out, one, rest
                ).astype(bf16)
        return own_at, pair_at, far_at

    starts = tuple(jnp.int32(g * LIST) for g in range(3))
    ends = lax.fori_loop(0, KT // GROUP, group, starts)
    for g in range(3):
        for u in range(UNROLL):
            todo[ends[g] + u] = 8 << 19
        todo[3 * LIST + g] = ends[g] - starts[g]


def left_products(a_tiles, p_tiles, col_ids, row_tiles, agg_ids, owner_map):
    rows = a_tiles.transpose(1, 0, 2).reshape(KT, RB, XP, 128)
    rows = rows.transpose(0, 2, 1, 3).reshape(KT * XP * RB, 128)
    vmem = pl.BlockSpec(memory_space=pltpu.VMEM)
    smem = pl.BlockSpec(memory_space=pltpu.SMEM)
    hbm = pl.BlockSpec(memory_space=pltpu.HBM)
    return pl.pallas_call(
        functools.partial(left_kernel, lax.axis_size("slab")),
        out_shape=[
            jax.ShapeDtypeStruct((TILES, CW, 128), bf16),
            jax.ShapeDtypeStruct((3 * LIST + 3,), jnp.int32),
        ],
        in_specs=[hbm] * 6,
        out_specs=[vmem, smem],
        scratch_shapes=[
            pltpu.VMEM((KT * XP * RB, 128), f32),
            pltpu.VMEM((RB, B * CW), f32),
            pltpu.VMEM((RB * XP, 128), f32),
            pltpu.VMEM((RB, CW, 256), bf16),
            pltpu.SMEM(col_ids.shape, jnp.int32),
            pltpu.SMEM(row_tiles.shape, jnp.int32),
            pltpu.SMEM(agg_ids.shape, jnp.int32),
            pltpu.SMEM(owner_map.shape, jnp.int32),
            pltpu.SemaphoreType.DMA((KT // GROUP,)),
            pltpu.SemaphoreType.DMA((5,)),
        ],
        compiler_params=pltpu.CompilerParams(vmem_limit_bytes=24 << 20),
        cost_estimate=pl.CostEstimate(
            flops=4_000_000_000, bytes_accessed=8_000_000, transcendentals=0
        ),
        name="left_products",
    )(*map(in_hbm, (rows, p_tiles, col_ids, row_tiles, agg_ids, owner_map)))


def right_kernel(which, sizes, n_after, *refs):
    n_slab, row_shift = sizes
    todo, aggs, t_ref, p_ref = refs[:4]
    refs = refs[4 + n_after :]
    outs = refs[: len(PLACES)]
    flat, panel, acc = refs[len(PLACES) :]
    row = lax.axis_index("row")
    slab = lax.axis_index("slab")
    if which == 0:
        near_slab = slab
    elif which == 1:
        near_slab = slab ^ 1
    else:
        near_slab = jnp.clip(slab + 2 * (slab & 1) - 1, 0, n_slab - 1)
    left = lax.broadcasted_iota(jnp.int32, (RB, 128), 1) < 64
    sub = lax.broadcasted_iota(jnp.int32, (RB, 128), 0)
    for b in range(N_ROW):
        near_row = (row + b) & (N_ROW - 1)
        odd = jnp.zeros((RB, 128), jnp.int32)
        for i in range(RB):
            odd = jnp.where(sub == i, aggs[near_row, 0, near_slab * RB + i], odd)
        odd = (odd & 1) == 1
        keep_even = jnp.logical_and(left, jnp.logical_not(odd))
        keep_odd = jnp.logical_and(jnp.logical_not(left), odd)
        for y in range(0, B, 2):
            v = p_ref[b * RB : (b + 1) * RB, y * 64 : y * 64 + 128]
            w = pltpu.roll(v, 64, 1)
            zero = jnp.zeros_like(v)
            flat[pl.ds(b * RB * B + y, RB, stride=B), :] = jnp.where(
                keep_even, v, jnp.where(keep_odd, w, zero)
            )
            flat[pl.ds(b * RB * B + y + 1, RB, stride=B), :] = jnp.where(
                keep_odd, v, jnp.where(keep_even, w, zero)
            )

    def prepare(m, carry):
        hi, lo = split(flat[pl.ds(pl.multiple_of(m * B, B), B), :])
        panel[m, :, :128] = hi
        panel[m, :, 128:] = lo
        return carry

    lax.fori_loop(0, N_ROW * RB, prepare, 0, unroll=4)
    acc[: 8 * PAIRS] = jnp.zeros((8 * PAIRS, CW, 128), f32)

    def step(n, carry):
        for u in range(UNROLL):
            entry = todo[which * LIST + n * UNROLL + u]
            source = (entry >> 8) & 2047
            source_row = source >> row_shift
            source_block = source & (RB - 1)
            source_slab = (source >> 3) & (n_slab - 1)
            pair = aggs[source_row, 0, source_slab * RB + source_block] >> 1
            at = ((source_row - row) & (N_ROW - 1)) * RB + source_block
            w = panel[at]
            o = jnp.dot(
                t_ref[entry & 255],
                jnp.concatenate([w, w], axis=0),
                preferred_element_type=f32,
            )
            acc[(entry >> 19) * PAIRS + pair] += o[:, :128] + o[:, 128:]
        return carry

    lax.fori_loop(0, (todo[3 * LIST + which] + UNROLL - 1) // UNROLL, step, 0)
    for out, places in zip(outs, PLACES, strict=True):
        for n, place in enumerate(places):
            out[n] = acc[place * PAIRS : (place + 1) * PAIRS]


def right_products(which, todo, agg_ids, t, panel, after=()):
    n_slab = lax.axis_size("slab")
    sizes = (n_slab, (RB * n_slab * lax.axis_size("col")).bit_length() - 1)
    vmem = pl.BlockSpec(memory_space=pltpu.VMEM)
    smem = pl.BlockSpec(memory_space=pltpu.SMEM)
    anywhere = pl.BlockSpec(memory_space=pl.ANY)
    return pl.pallas_call(
        functools.partial(right_kernel, which, sizes, len(after)),
        out_shape=[
            jax.ShapeDtypeStruct((len(places), PAIRS, CW, 128), f32)
            for places in PLACES
        ],
        in_specs=[smem, smem, vmem, vmem] + [anywhere] * len(after),
        out_specs=[vmem] * len(PLACES),
        scratch_shapes=[
            pltpu.VMEM((N_ROW * RB * B, 128), f32),
            pltpu.VMEM((N_ROW * RB, B, 256), bf16),
            pltpu.VMEM((9 * PAIRS, CW, 128), f32),
        ],
        compiler_params=pltpu.CompilerParams(vmem_limit_bytes=16 << 20),
        cost_estimate=pl.CostEstimate(
            flops=3_000_000_000, bytes_accessed=5_000_000, transcendentals=0
        ),
        name="right_products",
    )(todo, agg_ids, t, panel, *after)


def add_kernel(up_two, up_one, down_two, down_one, *refs):
    refs[-2][0] = up_two[0] + up_one[0]
    refs[-1][0] = down_two[0] + down_one[0]


def add_shares(up_two, up_one, down_two, down_one, after=()):
    vmem = pl.BlockSpec(memory_space=pltpu.VMEM)
    anywhere = pl.BlockSpec(memory_space=pl.ANY)
    return pl.pallas_call(
        add_kernel,
        out_shape=[jax.ShapeDtypeStruct((1, PAIRS, CW, 128), f32)] * 2,
        in_specs=[vmem] * 4 + [anywhere] * len(after),
        out_specs=[vmem] * 2,
        compiler_params=pltpu.CompilerParams(vmem_limit_bytes=2 << 20),
        name="add_shares",
    )(up_two, up_one, down_two, down_one, *after)


def finish_kernel(*refs):
    out = refs[-1]
    pair_is_upper = (lax.axis_index("slab") & 1) == 0
    upper, lower = 2 * PAIRS, 0
    firsts = [
        PAIRS,
        jnp.where(pair_is_upper, upper, lower),
        jnp.where(pair_is_upper, lower, upper),
    ]
    for g, first in enumerate(firsts):
        own, up_one, down_one, up_two, down_two = refs[5 * g : 5 * g + 5]
        for q in range(PAIRS):
            columns = pl.ds(pl.multiple_of((first + q) * 128, 128), 128)
            out[0, :, columns] = own[0, q] + down_one[1, q] + up_two[0, q]
            out[1, :, columns] = own[1, q] + up_one[1, q] + down_two[0, q]


def finish(parts):
    vmem = pl.BlockSpec(memory_space=pltpu.VMEM)
    return pl.pallas_call(
        finish_kernel,
        out_shape=jax.ShapeDtypeStruct((2, CW, 24 * CW), f32),
        in_specs=[vmem] * 15,
        out_specs=vmem,
        compiler_params=pltpu.CompilerParams(vmem_limit_bytes=24 << 20),
        name="finish",
    )(*parts)


def stack_kernel(*refs):
    out = refs[-1]
    for n, ref in enumerate(refs[:N_ROW]):
        out[n * RB : (n + 1) * RB, :] = ref[...]


def stack(blocks, after):
    vmem = pl.BlockSpec(memory_space=pltpu.VMEM)
    return pl.pallas_call(
        stack_kernel,
        out_shape=jax.ShapeDtypeStruct((N_ROW * RB, B * CW), f32),
        in_specs=[vmem] * N_ROW + [pl.BlockSpec(memory_space=pl.ANY)],
        out_specs=vmem,
        compiler_params=pltpu.CompilerParams(vmem_limit_bytes=2 << 20),
        name="stack",
    )(*blocks, after)


def on_device(a_tiles, p_tiles, col_ids, row_tiles, agg_ids, owner_map):
    n_slab = lax.axis_size("slab")
    ring = lambda step: [(i, (i + step) % N_ROW) for i in range(N_ROW)]
    twins = [(i, i ^ 1) for i in range(n_slab)]
    others = [
        (i, i + 2 * (i & 1) - 1)
        for i in range(n_slab)
        if 0 <= i + 2 * (i & 1) - 1 < n_slab
    ]
    up = lambda x: lax.ppermute(x, "row", ring(1))
    down = lambda x: lax.ppermute(x, "row", ring(-1))

    from_far = lax.ppermute(p_tiles, "row", ring(2))
    from_below = up(p_tiles)
    from_above = down(p_tiles)
    mid_blocks = [p_tiles, from_above, from_far, from_below]
    t, todo = left_products(
        a_tiles, p_tiles, col_ids, row_tiles, agg_ids, owner_map
    )
    stacked = stack(mid_blocks, todo)
    from_other = lax.ppermute(stacked, "slab", others)
    from_twin = lax.ppermute(stacked, "slab", twins)

    own = right_products(0, todo, agg_ids, t, stacked)
    own_up, own_down = up(own[1]), down(own[2])
    twin = right_products(1, todo, agg_ids, t, from_twin, (own[0],))
    twin_up, twin_down = up(twin[1]), down(twin[2])
    own_sums = add_shares(own[3], own_up, own[4], own_down, (twin[0],))
    own_two = up(own_sums[0]), down(own_sums[1])
    other = right_products(
        2, todo, agg_ids, t, from_other, (twin[0], own_sums[0])
    )
    other_up, other_down = up(other[1]), down(other[2])
    twin_sums = add_shares(twin[3], twin_up, twin[4], twin_down, (other[0],))
    twin_two = up(twin_sums[0]), down(twin_sums[1])
    other_sums = add_shares(
        other[3], other_up, other[4], other_down, (twin_sums[0],)
    )
    other_two = up(other_sums[0]), down(other_sums[1])
    out = finish(
        [own[0], own_up, own_down, *own_two]
        + [twin[0], twin_up, twin_down, *twin_two]
        + [other[0], other_up, other_down, *other_two]
    )
    return out.reshape(1, 1, 1, 2, CW, 24 * CW)


def solution(mesh):
    placed = (
        P(("row", "col", "slab"), None, None),
        P(("row", "col", "slab"), None),
        P(("row", "col", "slab"), None),
        P(("row", "col", "slab")),
        P(None, "col", None),
        P("col", "slab", None),
    )
    return jax.shard_map(
        on_device,
        mesh=mesh,
        in_specs=placed,
        out_specs=P("row", "col", "slab", None, None, None),
        check_vma=False,
    )
```

```python
import functools

import jax
import jax.numpy as jnp
from jax import lax
from jax.experimental import pallas as pl
from jax.experimental.pallas import tpu as pltpu
from jax.sharding import PartitionSpec as P

B = 64
CW = 64
KT = 27
RB = 8
NPOOL = 8
N_ROW = 4
UNROLL = 8
TILES = RB * KT
PAIRS = NPOOL // 2
LIST = TILES + UNROLL
GROUP = 3
XP = 32
PLACES = ((0, 1), (4, 3), (5, 6), (2,), (7,))
f32 = jnp.float32
bf16 = jnp.bfloat16


def split(x):
    hi = x.astype(bf16)
    return hi, (x - hi.astype(f32)).astype(bf16)


def in_hbm(x):
    return pltpu.with_memory_space_constraint(x, pltpu.HBM)


def left_kernel(
    n_slab,
    a_hbm,
    p_hbm,
    cols_hbm,
    counts_hbm,
    aggs_hbm,
    owners_hbm,
    t_ref,
    todo,
    a_buf,
    p_in,
    p_buf,
    lhs_buf,
    cols,
    counts,
    aggs,
    owners,
    a_sem,
    sem,
):
    small = [
        pltpu.make_async_copy(source, target, sem.at[n])
        for n, (source, target) in enumerate(
            [
                (p_hbm, p_in),
                (cols_hbm, cols),
                (counts_hbm, counts),
                (aggs_hbm, aggs),
                (owners_hbm, owners),
            ]
        )
    ]
    rows = GROUP * XP * RB

    def fetch(n):
        part = pl.ds(n * rows, rows)
        return pltpu.make_async_copy(a_hbm.at[part], a_buf.at[part], a_sem.at[n])

    for copy in small:
        copy.start()
    for n in range(KT // GROUP):
        fetch(n).start()
    for copy in small:
        copy.wait()
    row = lax.axis_index("row")
    slab = lax.axis_index("slab")
    for x in range(XP):
        p_buf[pl.ds(x, RB, stride=XP), :] = p_in[:, x * 128 : (x + 1) * 128]
    first = lax.broadcasted_iota(jnp.int32, (XP, 128), 1) < 64
    first_out = lax.broadcasted_iota(jnp.int32, (CW, 128), 1) < 64
    places = []
    for i in range(RB):
        packed = p_buf[i * XP : (i + 1) * XP, :]
        own = jnp.concatenate([packed[:, :64], packed[:, 64:]], axis=0)
        hi, lo = split(own.T)
        lhs_buf[i] = jnp.concatenate([hi, hi, lo, lo], axis=1)
        position = owners[0, 0, aggs[row, 0, slab * RB + i]]
        places.append((((position >> 1) - row) & (N_ROW - 1)) * 2 + (position & 1))

    def group(n, lengths):
        fetch(n).wait()
        own_at, pair_at, far_at = lengths
        entries = []
        for i in range(RB):
            for u in range(GROUP):
                k = n * GROUP + u
                source = cols[i, k]
                source_slab = (source >> 3) & (n_slab - 1)
                entries.append(
                    (
                        (source << 8) + (k * RB + i + (places[i] << 19)),
                        source_slab == slab,
                        source_slab == slab ^ 1,
                        k < counts[i],
                    )
                )
        for entry, is_own, is_pair, live in entries:
            todo[jnp.where(is_own, own_at, jnp.where(is_pair, pair_at, far_at))] = entry
            one = live.astype(jnp.int32)
            own_one = jnp.where(is_own, one, 0)
            pair_one = jnp.where(is_pair, one, 0)
            own_at = own_at + own_one
            pair_at = pair_at + pair_one
            far_at = far_at + (one - own_one - pair_one)
        for i in range(RB):
            lhs = lhs_buf[i]
            parts = []
            for u in range(GROUP):
                k = n * GROUP + u
                a = a_buf[pl.ds(k * (XP * RB) + i, XP, stride=RB), :]
                turned = pltpu.roll(a, 64, 1)
                two = jnp.concatenate(
                    [jnp.where(first, a, turned), jnp.where(first, turned, a)], axis=0
                )
                hi, lo = split(two)
                parts.append(jnp.concatenate([hi, lo, hi, lo], axis=0))

            t = jnp.dot(
                lhs, jnp.concatenate(parts, axis=1), preferred_element_type=f32
            )
            for u in range(GROUP):
                one = t[:, u * 128 : (u + 1) * 128]
                rest = one - one.astype(bf16).astype(f32)
                t_ref[(n * GROUP + u) * RB + i] = jnp.where(
                    first_out, one, rest
                ).astype(bf16)
        return own_at, pair_at, far_at

    starts = tuple(jnp.int32(g * LIST) for g in range(3))
    ends = lax.fori_loop(0, KT // GROUP, group, starts)
    for g in range(3):
        for u in range(UNROLL):
            todo[ends[g] + u] = 8 << 19
        todo[3 * LIST + g] = ends[g] - starts[g]


def left_products(a_tiles, p_tiles, col_ids, row_tiles, agg_ids, owner_map):
    rows = a_tiles.transpose(1, 0, 2).reshape(KT, RB, XP, 128)
    rows = rows.transpose(0, 2, 1, 3).reshape(KT * XP * RB, 128)
    vmem = pl.BlockSpec(memory_space=pltpu.VMEM)
    smem = pl.BlockSpec(memory_space=pltpu.SMEM)
    hbm = pl.BlockSpec(memory_space=pltpu.HBM)
    return pl.pallas_call(
        functools.partial(left_kernel, lax.axis_size("slab")),
        out_shape=[
            jax.ShapeDtypeStruct((TILES, CW, 128), bf16),
            jax.ShapeDtypeStruct((3 * LIST + 3,), jnp.int32),
        ],
        in_specs=[hbm] * 6,
        out_specs=[vmem, smem],
        scratch_shapes=[
            pltpu.VMEM((KT * XP * RB, 128), f32),
            pltpu.VMEM((RB, B * CW), f32),
            pltpu.VMEM((RB * XP, 128), f32),
            pltpu.VMEM((RB, CW, 256), bf16),
            pltpu.SMEM(col_ids.shape, jnp.int32),
            pltpu.SMEM(row_tiles.shape, jnp.int32),
            pltpu.SMEM(agg_ids.shape, jnp.int32),
            pltpu.SMEM(owner_map.shape, jnp.int32),
            pltpu.SemaphoreType.DMA((KT // GROUP,)),
            pltpu.SemaphoreType.DMA((5,)),
        ],
        compiler_params=pltpu.CompilerParams(vmem_limit_bytes=24 << 20),
        cost_estimate=pl.CostEstimate(
            flops=4_000_000_000, bytes_accessed=8_000_000, transcendentals=0
        ),
        name="left_products",
    )(*map(in_hbm, (rows, p_tiles, col_ids, row_tiles, agg_ids, owner_map)))


def right_kernel(which, sizes, n_after, *refs):
    n_slab, row_shift = sizes
    todo, aggs, t_ref, p_ref = refs[:4]
    refs = refs[4 + n_after :]
    outs = refs[: len(PLACES)]
    flat, panel, acc = refs[len(PLACES) :]
    row = lax.axis_index("row")
    slab = lax.axis_index("slab")
    if which == 0:
        near_slab = slab
    elif which == 1:
        near_slab = slab ^ 1
    else:
        near_slab = jnp.clip(slab + 2 * (slab & 1) - 1, 0, n_slab - 1)
    left = lax.broadcasted_iota(jnp.int32, (RB, 128), 1) < 64
    sub = lax.broadcasted_iota(jnp.int32, (RB, 128), 0)
    for b in range(N_ROW):
        near_row = (row + b) & (N_ROW - 1)
        odd = jnp.zeros((RB, 128), jnp.int32)
        for i in range(RB):
            odd = jnp.where(sub == i, aggs[near_row, 0, near_slab * RB + i], odd)
        odd = (odd & 1) == 1
        keep_even = jnp.logical_and(left, jnp.logical_not(odd))
        keep_odd = jnp.logical_and(jnp.logical_not(left), odd)
        for y in range(0, B, 2):
            v = p_ref[b * RB : (b + 1) * RB, y * 64 : y * 64 + 128]
            w = pltpu.roll(v, 64, 1)
            zero = jnp.zeros_like(v)
            flat[pl.ds(b * RB * B + y, RB, stride=B), :] = jnp.where(
                keep_even, v, jnp.where(keep_odd, w, zero)
            )
            flat[pl.ds(b * RB * B + y + 1, RB, stride=B), :] = jnp.where(
                keep_odd, v, jnp.where(keep_even, w, zero)
            )

    def prepare(m, carry):
        hi, lo = split(flat[pl.ds(pl.multiple_of(m * B, B), B), :])
        panel[m, :, :128] = hi
        panel[m, :, 128:] = lo
        return carry

    lax.fori_loop(0, N_ROW * RB, prepare, 0, unroll=4)
    acc[: 8 * PAIRS] = jnp.zeros((8 * PAIRS, CW, 128), f32)

    def step(n, carry):
        for u in range(UNROLL):
            entry = todo[which * LIST + n * UNROLL + u]
            source = (entry >> 8) & 2047
            source_row = source >> row_shift
            source_block = source & (RB - 1)
            source_slab = (source >> 3) & (n_slab - 1)
            pair = aggs[source_row, 0, source_slab * RB + source_block] >> 1
            at = ((source_row - row) & (N_ROW - 1)) * RB + source_block
            w = panel[at]
            o = jnp.dot(
                t_ref[entry & 255],
                jnp.concatenate([w, w], axis=0),
                preferred_element_type=f32,
            )
            acc[(entry >> 19) * PAIRS + pair] += o[:, :128] + o[:, 128:]
        return carry

    lax.fori_loop(0, (todo[3 * LIST + which] + UNROLL - 1) // UNROLL, step, 0)
    for out, places in zip(outs, PLACES, strict=True):
        for n, place in enumerate(places):
            out[n] = acc[place * PAIRS : (place + 1) * PAIRS]


def right_products(which, todo, agg_ids, t, panel, after=()):
    n_slab = lax.axis_size("slab")
    sizes = (n_slab, (RB * n_slab * lax.axis_size("col")).bit_length() - 1)
    vmem = pl.BlockSpec(memory_space=pltpu.VMEM)
    smem = pl.BlockSpec(memory_space=pltpu.SMEM)
    anywhere = pl.BlockSpec(memory_space=pl.ANY)
    return pl.pallas_call(
        functools.partial(right_kernel, which, sizes, len(after)),
        out_shape=[
            jax.ShapeDtypeStruct((len(places), PAIRS, CW, 128), f32)
            for places in PLACES
        ],
        in_specs=[smem, smem, vmem, vmem] + [anywhere] * len(after),
        out_specs=[vmem] * len(PLACES),
        scratch_shapes=[
            pltpu.VMEM((N_ROW * RB * B, 128), f32),
            pltpu.VMEM((N_ROW * RB, B, 256), bf16),
            pltpu.VMEM((9 * PAIRS, CW, 128), f32),
        ],
        compiler_params=pltpu.CompilerParams(vmem_limit_bytes=16 << 20),
        cost_estimate=pl.CostEstimate(
            flops=3_000_000_000, bytes_accessed=5_000_000, transcendentals=0
        ),
        name="right_products",
    )(todo, agg_ids, t, panel, *after)


def add_kernel(up_two, up_one, down_two, down_one, *refs):
    refs[-2][0] = up_two[0] + up_one[0]
    refs[-1][0] = down_two[0] + down_one[0]


def add_shares(up_two, up_one, down_two, down_one, after=()):
    vmem = pl.BlockSpec(memory_space=pltpu.VMEM)
    anywhere = pl.BlockSpec(memory_space=pl.ANY)
    return pl.pallas_call(
        add_kernel,
        out_shape=[jax.ShapeDtypeStruct((1, PAIRS, CW, 128), f32)] * 2,
        in_specs=[vmem] * 4 + [anywhere] * len(after),
        out_specs=[vmem] * 2,
        compiler_params=pltpu.CompilerParams(vmem_limit_bytes=2 << 20),
        name="add_shares",
    )(up_two, up_one, down_two, down_one, *after)


def finish_kernel(*refs):
    out = refs[-1]
    pair_is_upper = (lax.axis_index("slab") & 1) == 0
    upper, lower = 2 * PAIRS, 0
    firsts = [
        PAIRS,
        jnp.where(pair_is_upper, upper, lower),
        jnp.where(pair_is_upper, lower, upper),
    ]
    for g, first in enumerate(firsts):
        own, up_one, down_one, up_two, down_two = refs[5 * g : 5 * g + 5]
        for q in range(PAIRS):
            columns = pl.ds(pl.multiple_of((first + q) * 128, 128), 128)
            out[0, :, columns] = own[0, q] + down_one[1, q] + up_two[0, q]
            out[1, :, columns] = own[1, q] + up_one[1, q] + down_two[0, q]


def finish(parts):
    vmem = pl.BlockSpec(memory_space=pltpu.VMEM)
    return pl.pallas_call(
        finish_kernel,
        out_shape=jax.ShapeDtypeStruct((2, CW, 24 * CW), f32),
        in_specs=[vmem] * 15,
        out_specs=vmem,
        compiler_params=pltpu.CompilerParams(vmem_limit_bytes=24 << 20),
        name="finish",
    )(*parts)


def stack_kernel(*refs):
    out = refs[-1]
    for n, ref in enumerate(refs[:N_ROW]):
        out[n * RB : (n + 1) * RB, :] = ref[...]


def stack(blocks, after):
    vmem = pl.BlockSpec(memory_space=pltpu.VMEM)
    return pl.pallas_call(
        stack_kernel,
        out_shape=jax.ShapeDtypeStruct((N_ROW * RB, B * CW), f32),
        in_specs=[vmem] * N_ROW + [pl.BlockSpec(memory_space=pl.ANY)],
        out_specs=vmem,
        compiler_params=pltpu.CompilerParams(vmem_limit_bytes=2 << 20),
        name="stack",
    )(*blocks, after)


def on_device(a_tiles, p_tiles, col_ids, row_tiles, agg_ids, owner_map):
    n_slab = lax.axis_size("slab")
    ring = lambda step: [(i, (i + step) % N_ROW) for i in range(N_ROW)]
    twins = [(i, i ^ 1) for i in range(n_slab)]
    others = [
        (i, i + 2 * (i & 1) - 1)
        for i in range(n_slab)
        if 0 <= i + 2 * (i & 1) - 1 < n_slab
    ]
    up = lambda x: lax.ppermute(x, "row", ring(1))
    down = lambda x: lax.ppermute(x, "row", ring(-1))

    from_far = lax.ppermute(p_tiles, "row", ring(2))
    from_below = up(p_tiles)
    from_above = down(p_tiles)
    mid_blocks = [p_tiles, from_above, from_far, from_below]
    t, todo = left_products(
        a_tiles, p_tiles, col_ids, row_tiles, agg_ids, owner_map
    )
    stacked = stack(mid_blocks, todo)
    from_other = lax.ppermute(stacked, "slab", others)
    from_twin = lax.ppermute(stacked, "slab", twins)

    own = right_products(0, todo, agg_ids, t, stacked)
    own_up, own_down = up(own[1]), down(own[2])
    twin = right_products(1, todo, agg_ids, t, from_twin, (own[0],))
    twin_up, twin_down = up(twin[1]), down(twin[2])
    own_sums = add_shares(own[3], own_up, own[4], own_down, (twin[0],))
    own_two = up(own_sums[0]), down(own_sums[1])
    other = right_products(
        2, todo, agg_ids, t, from_other, (twin[0], own_sums[0])
    )
    other_up, other_down = up(other[1]), down(other[2])
    twin_sums = add_shares(twin[3], twin_up, twin[4], twin_down, (other[0],))
    twin_two = up(twin_sums[0]), down(twin_sums[1])
    other_sums = add_shares(
        other[3], other_up, other[4], other_down, (twin_two[0],)
    )
    other_two = up(other_sums[0]), down(other_sums[1])
    out = finish(
        [own[0], own_up, own_down, *own_two]
        + [twin[0], twin_up, twin_down, *twin_two]
        + [other[0], other_up, other_down, *other_two]
    )
    return out.reshape(1, 1, 1, 2, CW, 24 * CW)


def solution(mesh):
    placed = (
        P(("row", "col", "slab"), None, None),
        P(("row", "col", "slab"), None),
        P(("row", "col", "slab"), None),
        P(("row", "col", "slab")),
        P(None, "col", None),
        P("col", "slab", None),
    )
    return jax.shard_map(
        on_device,
        mesh=mesh,
        in_specs=placed,
        out_specs=P("row", "col", "slab", None, None, None),
        check_vma=False,
    )
```

```python
import functools

import jax
import jax.numpy as jnp
from jax import lax
from jax.experimental import pallas as pl
from jax.experimental.pallas import tpu as pltpu
from jax.sharding import PartitionSpec as P

B = 64
CW = 64
KT = 27
RB = 8
NPOOL = 8
N_ROW = 4
UNROLL = 8
TILES = RB * KT
PAIRS = NPOOL // 2
LIST = TILES + UNROLL
GROUP = 3
XP = 32
PLACES = ((0, 1), (4, 3), (5, 6), (2,), (7,))
f32 = jnp.float32
bf16 = jnp.bfloat16


def split(x):
    hi = x.astype(bf16)
    return hi, (x - hi.astype(f32)).astype(bf16)


def in_hbm(x):
    return pltpu.with_memory_space_constraint(x, pltpu.HBM)


def left_kernel(
    n_slab,
    a_hbm,
    p_hbm,
    cols_hbm,
    counts_hbm,
    aggs_hbm,
    owners_hbm,
    t_ref,
    todo,
    a_buf,
    p_in,
    p_buf,
    lhs_buf,
    cols,
    counts,
    aggs,
    owners,
    a_sem,
    sem,
):
    small = [
        pltpu.make_async_copy(source, target, sem.at[n])
        for n, (source, target) in enumerate(
            [
                (p_hbm, p_in),
                (cols_hbm, cols),
                (counts_hbm, counts),
                (aggs_hbm, aggs),
                (owners_hbm, owners),
            ]
        )
    ]
    rows = GROUP * XP * RB

    def fetch(n):
        part = pl.ds(n * rows, rows)
        return pltpu.make_async_copy(a_hbm.at[part], a_buf.at[part], a_sem.at[n])

    for copy in small:
        copy.start()
    for n in range(KT // GROUP):
        fetch(n).start()
    for copy in small:
        copy.wait()
    row = lax.axis_index("row")
    slab = lax.axis_index("slab")
    for x in range(XP):
        p_buf[pl.ds(x, RB, stride=XP), :] = p_in[:, x * 128 : (x + 1) * 128]
    first = lax.broadcasted_iota(jnp.int32, (XP, 128), 1) < 64
    first_out = lax.broadcasted_iota(jnp.int32, (CW, 128), 1) < 64
    places = []
    for i in range(RB):
        packed = p_buf[i * XP : (i + 1) * XP, :]
        own = jnp.concatenate([packed[:, :64], packed[:, 64:]], axis=0)
        hi, lo = split(own.T)
        lhs_buf[i] = jnp.concatenate([hi, hi, lo, lo], axis=1)
        position = owners[0, 0, aggs[row, 0, slab * RB + i]]
        places.append((((position >> 1) - row) & (N_ROW - 1)) * 2 + (position & 1))

    def group(n, lengths):
        fetch(n).wait()
        own_at, pair_at, far_at = lengths
        entries = []
        for i in range(RB):
            for u in range(GROUP):
                k = n * GROUP + u
                source = cols[i, k]
                source_slab = (source >> 3) & (n_slab - 1)
                entries.append(
                    (
                        (source << 8) + (k * RB + i + (places[i] << 19)),
                        source_slab == slab,
                        source_slab == slab ^ 1,
                        k < counts[i],
                    )
                )
        for i in range(RB):
            lhs = lhs_buf[i]
            parts = []
            for u in range(GROUP):
                k = n * GROUP + u
                a = a_buf[pl.ds(k * (XP * RB) + i, XP, stride=RB), :]
                turned = pltpu.roll(a, 64, 1)
                two = jnp.concatenate(
                    [jnp.where(first, a, turned), jnp.where(first, turned, a)], axis=0
                )
                hi, lo = split(two)
                parts.append(jnp.concatenate([hi, lo, hi, lo], axis=0))

            t = jnp.dot(
                lhs, jnp.concatenate(parts, axis=1), preferred_element_type=f32
            )
            for u in range(GROUP):
                one = t[:, u * 128 : (u + 1) * 128]
                rest = one - one.astype(bf16).astype(f32)
                t_ref[(n * GROUP + u) * RB + i] = jnp.where(
                    first_out, one, rest
                ).astype(bf16)
        for entry, is_own, is_pair, live in entries:
            todo[jnp.where(is_own, own_at, jnp.where(is_pair, pair_at, far_at))] = entry
            one = live.astype(jnp.int32)
            own_one = jnp.where(is_own, one, 0)
            pair_one = jnp.where(is_pair, one, 0)
            own_at = own_at + own_one
            pair_at = pair_at + pair_one
            far_at = far_at + (one - own_one - pair_one)
        return own_at, pair_at, far_at

    starts = tuple(jnp.int32(g * LIST) for g in range(3))
    ends = lax.fori_loop(0, KT // GROUP, group, starts)
    for g in range(3):
        for u in range(UNROLL):
            todo[ends[g] + u] = 8 << 19
        todo[3 * LIST + g] = ends[g] - starts[g]


def left_products(a_tiles, p_tiles, col_ids, row_tiles, agg_ids, owner_map):
    rows = a_tiles.transpose(1, 0, 2).reshape(KT, RB, XP, 128)
    rows = rows.transpose(0, 2, 1, 3).reshape(KT * XP * RB, 128)
    vmem = pl.BlockSpec(memory_space=pltpu.VMEM)
    smem = pl.BlockSpec(memory_space=pltpu.SMEM)
    hbm = pl.BlockSpec(memory_space=pltpu.HBM)
    return pl.pallas_call(
        functools.partial(left_kernel, lax.axis_size("slab")),
        out_shape=[
            jax.ShapeDtypeStruct((TILES, CW, 128), bf16),
            jax.ShapeDtypeStruct((3 * LIST + 3,), jnp.int32),
        ],
        in_specs=[hbm] * 6,
        out_specs=[vmem, smem],
        scratch_shapes=[
            pltpu.VMEM((KT * XP * RB, 128), f32),
            pltpu.VMEM((RB, B * CW), f32),
            pltpu.VMEM((RB * XP, 128), f32),
            pltpu.VMEM((RB, CW, 256), bf16),
            pltpu.SMEM(col_ids.shape, jnp.int32),
            pltpu.SMEM(row_tiles.shape, jnp.int32),
            pltpu.SMEM(agg_ids.shape, jnp.int32),
            pltpu.SMEM(owner_map.shape, jnp.int32),
            pltpu.SemaphoreType.DMA((KT // GROUP,)),
            pltpu.SemaphoreType.DMA((5,)),
        ],
        compiler_params=pltpu.CompilerParams(vmem_limit_bytes=24 << 20),
        cost_estimate=pl.CostEstimate(
            flops=4_000_000_000, bytes_accessed=8_000_000, transcendentals=0
        ),
        name="left_products",
    )(*map(in_hbm, (rows, p_tiles, col_ids, row_tiles, agg_ids, owner_map)))


def right_kernel(which, sizes, n_after, *refs):
    n_slab, row_shift = sizes
    todo, aggs, t_ref, p_ref = refs[:4]
    refs = refs[4 + n_after :]
    outs = refs[: len(PLACES)]
    flat, panel, acc = refs[len(PLACES) :]
    row = lax.axis_index("row")
    slab = lax.axis_index("slab")
    if which == 0:
        near_slab = slab
    elif which == 1:
        near_slab = slab ^ 1
    else:
        near_slab = jnp.clip(slab + 2 * (slab & 1) - 1, 0, n_slab - 1)
    left = lax.broadcasted_iota(jnp.int32, (RB, 128), 1) < 64
    sub = lax.broadcasted_iota(jnp.int32, (RB, 128), 0)
    for b in range(N_ROW):
        near_row = (row + b) & (N_ROW - 1)
        odd = jnp.zeros((RB, 128), jnp.int32)
        for i in range(RB):
            odd = jnp.where(sub == i, aggs[near_row, 0, near_slab * RB + i], odd)
        odd = (odd & 1) == 1
        keep_even = jnp.logical_and(left, jnp.logical_not(odd))
        keep_odd = jnp.logical_and(jnp.logical_not(left), odd)
        for y in range(0, B, 2):
            v = p_ref[b * RB : (b + 1) * RB, y * 64 : y * 64 + 128]
            w = pltpu.roll(v, 64, 1)
            zero = jnp.zeros_like(v)
            flat[pl.ds(b * RB * B + y, RB, stride=B), :] = jnp.where(
                keep_even, v, jnp.where(keep_odd, w, zero)
            )
            flat[pl.ds(b * RB * B + y + 1, RB, stride=B), :] = jnp.where(
                keep_odd, v, jnp.where(keep_even, w, zero)
            )

    def prepare(m, carry):
        hi, lo = split(flat[pl.ds(pl.multiple_of(m * B, B), B), :])
        panel[m, :, :128] = hi
        panel[m, :, 128:] = lo
        return carry

    lax.fori_loop(0, N_ROW * RB, prepare, 0, unroll=4)
    acc[: 8 * PAIRS] = jnp.zeros((8 * PAIRS, CW, 128), f32)

    def step(n, carry):
        for u in range(UNROLL):
            entry = todo[which * LIST + n * UNROLL + u]
            source = (entry >> 8) & 2047
            source_row = source >> row_shift
            source_block = source & (RB - 1)
            source_slab = (source >> 3) & (n_slab - 1)
            pair = aggs[source_row, 0, source_slab * RB + source_block] >> 1
            at = ((source_row - row) & (N_ROW - 1)) * RB + source_block
            w = panel[at]
            o = jnp.dot(
                t_ref[entry & 255],
                jnp.concatenate([w, w], axis=0),
                preferred_element_type=f32,
            )
            acc[(entry >> 19) * PAIRS + pair] += o[:, :128] + o[:, 128:]
        return carry

    lax.fori_loop(0, (todo[3 * LIST + which] + UNROLL - 1) // UNROLL, step, 0)
    for out, places in zip(outs, PLACES, strict=True):
        for n, place in enumerate(places):
            out[n] = acc[place * PAIRS : (place + 1) * PAIRS]


def right_products(which, todo, agg_ids, t, panel, after=()):
    n_slab = lax.axis_size("slab")
    sizes = (n_slab, (RB * n_slab * lax.axis_size("col")).bit_length() - 1)
    vmem = pl.BlockSpec(memory_space=pltpu.VMEM)
    smem = pl.BlockSpec(memory_space=pltpu.SMEM)
    anywhere = pl.BlockSpec(memory_space=pl.ANY)
    return pl.pallas_call(
        functools.partial(right_kernel, which, sizes, len(after)),
        out_shape=[
            jax.ShapeDtypeStruct((len(places), PAIRS, CW, 128), f32)
            for places in PLACES
        ],
        in_specs=[smem, smem, vmem, vmem] + [anywhere] * len(after),
        out_specs=[vmem] * len(PLACES),
        scratch_shapes=[
            pltpu.VMEM((N_ROW * RB * B, 128), f32),
            pltpu.VMEM((N_ROW * RB, B, 256), bf16),
            pltpu.VMEM((9 * PAIRS, CW, 128), f32),
        ],
        compiler_params=pltpu.CompilerParams(vmem_limit_bytes=16 << 20),
        cost_estimate=pl.CostEstimate(
            flops=3_000_000_000, bytes_accessed=5_000_000, transcendentals=0
        ),
        name="right_products",
    )(todo, agg_ids, t, panel, *after)


def add_kernel(up_two, up_one, down_two, down_one, *refs):
    refs[-2][0] = up_two[0] + up_one[0]
    refs[-1][0] = down_two[0] + down_one[0]


def add_shares(up_two, up_one, down_two, down_one, after=()):
    vmem = pl.BlockSpec(memory_space=pltpu.VMEM)
    anywhere = pl.BlockSpec(memory_space=pl.ANY)
    return pl.pallas_call(
        add_kernel,
        out_shape=[jax.ShapeDtypeStruct((1, PAIRS, CW, 128), f32)] * 2,
        in_specs=[vmem] * 4 + [anywhere] * len(after),
        out_specs=[vmem] * 2,
        compiler_params=pltpu.CompilerParams(vmem_limit_bytes=2 << 20),
        name="add_shares",
    )(up_two, up_one, down_two, down_one, *after)


def finish_kernel(*refs):
    out = refs[-1]
    pair_is_upper = (lax.axis_index("slab") & 1) == 0
    upper, lower = 2 * PAIRS, 0
    firsts = [
        PAIRS,
        jnp.where(pair_is_upper, upper, lower),
        jnp.where(pair_is_upper, lower, upper),
    ]
    for g, first in enumerate(firsts):
        own, up_one, down_one, up_two, down_two = refs[5 * g : 5 * g + 5]
        for q in range(PAIRS):
            columns = pl.ds(pl.multiple_of((first + q) * 128, 128), 128)
            out[0, :, columns] = own[0, q] + down_one[1, q] + up_two[0, q]
            out[1, :, columns] = own[1, q] + up_one[1, q] + down_two[0, q]


def finish(parts):
    vmem = pl.BlockSpec(memory_space=pltpu.VMEM)
    return pl.pallas_call(
        finish_kernel,
        out_shape=jax.ShapeDtypeStruct((2, CW, 24 * CW), f32),
        in_specs=[vmem] * 15,
        out_specs=vmem,
        compiler_params=pltpu.CompilerParams(vmem_limit_bytes=24 << 20),
        name="finish",
    )(*parts)


def stack_kernel(*refs):
    out = refs[-1]
    for n, ref in enumerate(refs[:N_ROW]):
        out[n * RB : (n + 1) * RB, :] = ref[...]


def stack(blocks, after):
    vmem = pl.BlockSpec(memory_space=pltpu.VMEM)
    return pl.pallas_call(
        stack_kernel,
        out_shape=jax.ShapeDtypeStruct((N_ROW * RB, B * CW), f32),
        in_specs=[vmem] * N_ROW + [pl.BlockSpec(memory_space=pl.ANY)],
        out_specs=vmem,
        compiler_params=pltpu.CompilerParams(vmem_limit_bytes=2 << 20),
        name="stack",
    )(*blocks, after)


def on_device(a_tiles, p_tiles, col_ids, row_tiles, agg_ids, owner_map):
    n_slab = lax.axis_size("slab")
    ring = lambda step: [(i, (i + step) % N_ROW) for i in range(N_ROW)]
    twins = [(i, i ^ 1) for i in range(n_slab)]
    others = [
        (i, i + 2 * (i & 1) - 1)
        for i in range(n_slab)
        if 0 <= i + 2 * (i & 1) - 1 < n_slab
    ]
    up = lambda x: lax.ppermute(x, "row", ring(1))
    down = lambda x: lax.ppermute(x, "row", ring(-1))

    from_far = lax.ppermute(p_tiles, "row", ring(2))
    from_below = up(p_tiles)
    from_above = down(p_tiles)
    mid_blocks = [p_tiles, from_above, from_far, from_below]
    t, todo = left_products(
        a_tiles, p_tiles, col_ids, row_tiles, agg_ids, owner_map
    )
    stacked = stack(mid_blocks, todo)
    from_other = lax.ppermute(stacked, "slab", others)
    from_twin = lax.ppermute(stacked, "slab", twins)

    own = right_products(0, todo, agg_ids, t, stacked)
    own_up, own_down = up(own[1]), down(own[2])
    twin = right_products(1, todo, agg_ids, t, from_twin, (own[0],))
    twin_up, twin_down = up(twin[1]), down(twin[2])
    own_sums = add_shares(own[3], own_up, own[4], own_down, (twin[0],))
    own_two = up(own_sums[0]), down(own_sums[1])
    other = right_products(
        2, todo, agg_ids, t, from_other, (twin[0], own_sums[0])
    )
    other_up, other_down = up(other[1]), down(other[2])
    twin_sums = add_shares(twin[3], twin_up, twin[4], twin_down, (other[0],))
    twin_two = up(twin_sums[0]), down(twin_sums[1])
    other_sums = add_shares(
        other[3], other_up, other[4], other_down, (twin_two[0],)
    )
    other_two = up(other_sums[0]), down(other_sums[1])
    out = finish(
        [own[0], own_up, own_down, *own_two]
        + [twin[0], twin_up, twin_down, *twin_two]
        + [other[0], other_up, other_down, *other_two]
    )
    return out.reshape(1, 1, 1, 2, CW, 24 * CW)


def solution(mesh):
    placed = (
        P(("row", "col", "slab"), None, None),
        P(("row", "col", "slab"), None),
        P(("row", "col", "slab"), None),
        P(("row", "col", "slab")),
        P(None, "col", None),
        P("col", "slab", None),
    )
    return jax.shard_map(
        on_device,
        mesh=mesh,
        in_specs=placed,
        out_specs=P("row", "col", "slab", None, None, None),
        check_vma=False,
    )
```

```python
import functools

import jax
import jax.numpy as jnp
from jax import lax
from jax.experimental import pallas as pl
from jax.experimental.pallas import tpu as pltpu
from jax.sharding import PartitionSpec as P

B = 64
CW = 64
KT = 27
RB = 8
NPOOL = 8
N_ROW = 4
UNROLL = 8
TILES = RB * KT
PAIRS = NPOOL // 2
LIST = TILES + UNROLL
GROUP = 9
XP = 32
PLACES = ((0, 1), (4, 3), (5, 6), (2,), (7,))
f32 = jnp.float32
bf16 = jnp.bfloat16


def split(x):
    hi = x.astype(bf16)
    return hi, (x - hi.astype(f32)).astype(bf16)


def in_hbm(x):
    return pltpu.with_memory_space_constraint(x, pltpu.HBM)


def left_kernel(
    n_slab,
    a_hbm,
    p_hbm,
    cols_hbm,
    counts_hbm,
    aggs_hbm,
    owners_hbm,
    t_ref,
    todo,
    a_buf,
    p_in,
    p_buf,
    lhs_buf,
    cols,
    counts,
    aggs,
    owners,
    a_sem,
    sem,
):
    small = [
        pltpu.make_async_copy(source, target, sem.at[n])
        for n, (source, target) in enumerate(
            [
                (p_hbm, p_in),
                (cols_hbm, cols),
                (counts_hbm, counts),
                (aggs_hbm, aggs),
                (owners_hbm, owners),
            ]
        )
    ]
    rows = GROUP * XP * RB

    def fetch(n):
        part = pl.ds(n * rows, rows)
        return pltpu.make_async_copy(a_hbm.at[part], a_buf.at[part], a_sem.at[n])

    for copy in small:
        copy.start()
    for n in range(KT // GROUP):
        fetch(n).start()
    for copy in small:
        copy.wait()
    row = lax.axis_index("row")
    slab = lax.axis_index("slab")
    for x in range(XP):
        p_buf[pl.ds(x, RB, stride=XP), :] = p_in[:, x * 128 : (x + 1) * 128]
    first = lax.broadcasted_iota(jnp.int32, (XP, 128), 1) < 64
    first_out = lax.broadcasted_iota(jnp.int32, (CW, 128), 1) < 64
    places = []
    for i in range(RB):
        packed = p_buf[i * XP : (i + 1) * XP, :]
        own = jnp.concatenate([packed[:, :64], packed[:, 64:]], axis=0)
        hi, lo = split(own.T)
        lhs_buf[i] = jnp.concatenate([hi, hi, lo, lo], axis=1)
        position = owners[0, 0, aggs[row, 0, slab * RB + i]]
        places.append((((position >> 1) - row) & (N_ROW - 1)) * 2 + (position & 1))

    def group(n, lengths):
        fetch(n).wait()
        own_at, pair_at, far_at = lengths
        entries = []
        for i in range(RB):
            for u in range(GROUP):
                k = n * GROUP + u
                source = cols[i, k]
                source_slab = (source >> 3) & (n_slab - 1)
                entries.append(
                    (
                        (source << 8) + (k * RB + i + (places[i] << 19)),
                        source_slab == slab,
                        source_slab == slab ^ 1,
                        k < counts[i],
                    )
                )
        for i in range(RB):
            lhs = lhs_buf[i]
            parts = []
            for u in range(GROUP):
                k = n * GROUP + u
                a = a_buf[pl.ds(k * (XP * RB) + i, XP, stride=RB), :]
                turned = pltpu.roll(a, 64, 1)
                two = jnp.concatenate(
                    [jnp.where(first, a, turned), jnp.where(first, turned, a)], axis=0
                )
                hi, lo = split(two)
                parts.append(jnp.concatenate([hi, lo, hi, lo], axis=0))

            t = jnp.dot(
                lhs, jnp.concatenate(parts, axis=1), preferred_element_type=f32
            )
            for u in range(GROUP):
                one = t[:, u * 128 : (u + 1) * 128]
                rest = one - one.astype(bf16).astype(f32)
                t_ref[(n * GROUP + u) * RB + i] = jnp.where(
                    first_out, one, rest
                ).astype(bf16)
        for entry, is_own, is_pair, live in entries:
            todo[jnp.where(is_own, own_at, jnp.where(is_pair, pair_at, far_at))] = entry
            one = live.astype(jnp.int32)
            own_one = jnp.where(is_own, one, 0)
            pair_one = jnp.where(is_pair, one, 0)
            own_at = own_at + own_one
            pair_at = pair_at + pair_one
            far_at = far_at + (one - own_one - pair_one)
        return own_at, pair_at, far_at

    starts = tuple(jnp.int32(g * LIST) for g in range(3))
    ends = lax.fori_loop(0, KT // GROUP, group, starts)
    for g in range(3):
        for u in range(UNROLL):
            todo[ends[g] + u] = 8 << 19
        todo[3 * LIST + g] = ends[g] - starts[g]


def left_products(a_tiles, p_tiles, col_ids, row_tiles, agg_ids, owner_map):
    rows = a_tiles.transpose(1, 0, 2).reshape(KT, RB, XP, 128)
    rows = rows.transpose(0, 2, 1, 3).reshape(KT * XP * RB, 128)
    vmem = pl.BlockSpec(memory_space=pltpu.VMEM)
    smem = pl.BlockSpec(memory_space=pltpu.SMEM)
    hbm = pl.BlockSpec(memory_space=pltpu.HBM)
    return pl.pallas_call(
        functools.partial(left_kernel, lax.axis_size("slab")),
        out_shape=[
            jax.ShapeDtypeStruct((TILES, CW, 128), bf16),
            jax.ShapeDtypeStruct((3 * LIST + 3,), jnp.int32),
        ],
        in_specs=[hbm] * 6,
        out_specs=[vmem, smem],
        scratch_shapes=[
            pltpu.VMEM((KT * XP * RB, 128), f32),
            pltpu.VMEM((RB, B * CW), f32),
            pltpu.VMEM((RB * XP, 128), f32),
            pltpu.VMEM((RB, CW, 256), bf16),
            pltpu.SMEM(col_ids.shape, jnp.int32),
            pltpu.SMEM(row_tiles.shape, jnp.int32),
            pltpu.SMEM(agg_ids.shape, jnp.int32),
            pltpu.SMEM(owner_map.shape, jnp.int32),
            pltpu.SemaphoreType.DMA((KT // GROUP,)),
            pltpu.SemaphoreType.DMA((5,)),
        ],
        compiler_params=pltpu.CompilerParams(vmem_limit_bytes=24 << 20),
        cost_estimate=pl.CostEstimate(
            flops=4_000_000_000, bytes_accessed=8_000_000, transcendentals=0
        ),
        name="left_products",
    )(*map(in_hbm, (rows, p_tiles, col_ids, row_tiles, agg_ids, owner_map)))


def right_kernel(which, sizes, n_after, *refs):
    n_slab, row_shift = sizes
    todo, aggs, t_ref, p_ref = refs[:4]
    refs = refs[4 + n_after :]
    outs = refs[: len(PLACES)]
    flat, panel, acc = refs[len(PLACES) :]
    row = lax.axis_index("row")
    slab = lax.axis_index("slab")
    if which == 0:
        near_slab = slab
    elif which == 1:
        near_slab = slab ^ 1
    else:
        near_slab = jnp.clip(slab + 2 * (slab & 1) - 1, 0, n_slab - 1)
    left = lax.broadcasted_iota(jnp.int32, (RB, 128), 1) < 64
    sub = lax.broadcasted_iota(jnp.int32, (RB, 128), 0)
    for b in range(N_ROW):
        near_row = (row + b) & (N_ROW - 1)
        odd = jnp.zeros((RB, 128), jnp.int32)
        for i in range(RB):
            odd = jnp.where(sub == i, aggs[near_row, 0, near_slab * RB + i], odd)
        odd = (odd & 1) == 1
        keep_even = jnp.logical_and(left, jnp.logical_not(odd))
        keep_odd = jnp.logical_and(jnp.logical_not(left), odd)
        for y in range(0, B, 2):
            v = p_ref[b * RB : (b + 1) * RB, y * 64 : y * 64 + 128]
            w = pltpu.roll(v, 64, 1)
            zero = jnp.zeros_like(v)
            flat[pl.ds(b * RB * B + y, RB, stride=B), :] = jnp.where(
                keep_even, v, jnp.where(keep_odd, w, zero)
            )
            flat[pl.ds(b * RB * B + y + 1, RB, stride=B), :] = jnp.where(
                keep_odd, v, jnp.where(keep_even, w, zero)
            )

    def prepare(m, carry):
        hi, lo = split(flat[pl.ds(pl.multiple_of(m * B, B), B), :])
        panel[m, :, :128] = hi
        panel[m, :, 128:] = lo
        return carry

    lax.fori_loop(0, N_ROW * RB, prepare, 0, unroll=4)
    acc[: 8 * PAIRS] = jnp.zeros((8 * PAIRS, CW, 128), f32)

    def step(n, carry):
        for u in range(UNROLL):
            entry = todo[which * LIST + n * UNROLL + u]
            source = (entry >> 8) & 2047
            source_row = source >> row_shift
            source_block = source & (RB - 1)
            source_slab = (source >> 3) & (n_slab - 1)
            pair = aggs[source_row, 0, source_slab * RB + source_block] >> 1
            at = ((source_row - row) & (N_ROW - 1)) * RB + source_block
            w = panel[at]
            o = jnp.dot(
                t_ref[entry & 255],
                jnp.concatenate([w, w], axis=0),
                preferred_element_type=f32,
            )
            acc[(entry >> 19) * PAIRS + pair] += o[:, :128] + o[:, 128:]
        return carry

    lax.fori_loop(0, (todo[3 * LIST + which] + UNROLL - 1) // UNROLL, step, 0)
    for out, places in zip(outs, PLACES, strict=True):
        for n, place in enumerate(places):
            out[n] = acc[place * PAIRS : (place + 1) * PAIRS]


def right_products(which, todo, agg_ids, t, panel, after=()):
    n_slab = lax.axis_size("slab")
    sizes = (n_slab, (RB * n_slab * lax.axis_size("col")).bit_length() - 1)
    vmem = pl.BlockSpec(memory_space=pltpu.VMEM)
    smem = pl.BlockSpec(memory_space=pltpu.SMEM)
    anywhere = pl.BlockSpec(memory_space=pl.ANY)
    return pl.pallas_call(
        functools.partial(right_kernel, which, sizes, len(after)),
        out_shape=[
            jax.ShapeDtypeStruct((len(places), PAIRS, CW, 128), f32)
            for places in PLACES
        ],
        in_specs=[smem, smem, vmem, vmem] + [anywhere] * len(after),
        out_specs=[vmem] * len(PLACES),
        scratch_shapes=[
            pltpu.VMEM((N_ROW * RB * B, 128), f32),
            pltpu.VMEM((N_ROW * RB, B, 256), bf16),
            pltpu.VMEM((9 * PAIRS, CW, 128), f32),
        ],
        compiler_params=pltpu.CompilerParams(vmem_limit_bytes=16 << 20),
        cost_estimate=pl.CostEstimate(
            flops=3_000_000_000, bytes_accessed=5_000_000, transcendentals=0
        ),
        name="right_products",
    )(todo, agg_ids, t, panel, *after)


def add_kernel(up_two, up_one, down_two, down_one, *refs):
    refs[-2][0] = up_two[0] + up_one[0]
    refs[-1][0] = down_two[0] + down_one[0]


def add_shares(up_two, up_one, down_two, down_one, after=()):
    vmem = pl.BlockSpec(memory_space=pltpu.VMEM)
    anywhere = pl.BlockSpec(memory_space=pl.ANY)
    return pl.pallas_call(
        add_kernel,
        out_shape=[jax.ShapeDtypeStruct((1, PAIRS, CW, 128), f32)] * 2,
        in_specs=[vmem] * 4 + [anywhere] * len(after),
        out_specs=[vmem] * 2,
        compiler_params=pltpu.CompilerParams(vmem_limit_bytes=2 << 20),
        name="add_shares",
    )(up_two, up_one, down_two, down_one, *after)


def finish_kernel(*refs):
    out = refs[-1]
    pair_is_upper = (lax.axis_index("slab") & 1) == 0
    upper, lower = 2 * PAIRS, 0
    firsts = [
        PAIRS,
        jnp.where(pair_is_upper, upper, lower),
        jnp.where(pair_is_upper, lower, upper),
    ]
    for g, first in enumerate(firsts):
        own, up_one, down_one, up_two, down_two = refs[5 * g : 5 * g + 5]
        for q in range(PAIRS):
            columns = pl.ds(pl.multiple_of((first + q) * 128, 128), 128)
            out[0, :, columns] = own[0, q] + down_one[1, q] + up_two[0, q]
            out[1, :, columns] = own[1, q] + up_one[1, q] + down_two[0, q]


def finish(parts):
    vmem = pl.BlockSpec(memory_space=pltpu.VMEM)
    return pl.pallas_call(
        finish_kernel,
        out_shape=jax.ShapeDtypeStruct((2, CW, 24 * CW), f32),
        in_specs=[vmem] * 15,
        out_specs=vmem,
        compiler_params=pltpu.CompilerParams(vmem_limit_bytes=24 << 20),
        name="finish",
    )(*parts)


def stack_kernel(*refs):
    out = refs[-1]
    for n, ref in enumerate(refs[:N_ROW]):
        out[n * RB : (n + 1) * RB, :] = ref[...]


def stack(blocks, after):
    vmem = pl.BlockSpec(memory_space=pltpu.VMEM)
    return pl.pallas_call(
        stack_kernel,
        out_shape=jax.ShapeDtypeStruct((N_ROW * RB, B * CW), f32),
        in_specs=[vmem] * N_ROW + [pl.BlockSpec(memory_space=pl.ANY)],
        out_specs=vmem,
        compiler_params=pltpu.CompilerParams(vmem_limit_bytes=2 << 20),
        name="stack",
    )(*blocks, after)


def on_device(a_tiles, p_tiles, col_ids, row_tiles, agg_ids, owner_map):
    n_slab = lax.axis_size("slab")
    ring = lambda step: [(i, (i + step) % N_ROW) for i in range(N_ROW)]
    twins = [(i, i ^ 1) for i in range(n_slab)]
    others = [
        (i, i + 2 * (i & 1) - 1)
        for i in range(n_slab)
        if 0 <= i + 2 * (i & 1) - 1 < n_slab
    ]
    up = lambda x: lax.ppermute(x, "row", ring(1))
    down = lambda x: lax.ppermute(x, "row", ring(-1))

    from_far = lax.ppermute(p_tiles, "row", ring(2))
    from_below = up(p_tiles)
    from_above = down(p_tiles)
    mid_blocks = [p_tiles, from_above, from_far, from_below]
    t, todo = left_products(
        a_tiles, p_tiles, col_ids, row_tiles, agg_ids, owner_map
    )
    stacked = stack(mid_blocks, todo)
    from_other = lax.ppermute(stacked, "slab", others)
    from_twin = lax.ppermute(stacked, "slab", twins)

    own = right_products(0, todo, agg_ids, t, stacked)
    own_up, own_down = up(own[1]), down(own[2])
    twin = right_products(1, todo, agg_ids, t, from_twin, (own[0],))
    twin_up, twin_down = up(twin[1]), down(twin[2])
    own_sums = add_shares(own[3], own_up, own[4], own_down, (twin[0],))
    own_two = up(own_sums[0]), down(own_sums[1])
    other = right_products(
        2, todo, agg_ids, t, from_other, (twin[0], own_sums[0])
    )
    other_up, other_down = up(other[1]), down(other[2])
    twin_sums = add_shares(twin[3], twin_up, twin[4], twin_down, (other[0],))
    twin_two = up(twin_sums[0]), down(twin_sums[1])
    other_sums = add_shares(
        other[3], other_up, other[4], other_down, (twin_two[0],)
    )
    other_two = up(other_sums[0]), down(other_sums[1])
    out = finish(
        [own[0], own_up, own_down, *own_two]
        + [twin[0], twin_up, twin_down, *twin_two]
        + [other[0], other_up, other_down, *other_two]
    )
    return out.reshape(1, 1, 1, 2, CW, 24 * CW)


def solution(mesh):
    placed = (
        P(("row", "col", "slab"), None, None),
        P(("row", "col", "slab"), None),
        P(("row", "col", "slab"), None),
        P(("row", "col", "slab")),
        P(None, "col", None),
        P("col", "slab", None),
    )
    return jax.shard_map(
        on_device,
        mesh=mesh,
        in_specs=placed,
        out_specs=P("row", "col", "slab", None, None, None),
        check_vma=False,
    )
```
